32 devices in a mesh: ctx: 16 (over z, y, x), head: 2 (over core).
Axes of the slice: x: 2, y: 2, z: 4, core: 2. Of those that a mesh axis runs over, the one named last changes fastest.
Arguments:
- obs_query: bfloat16 [256, 5120], P('ctx', 'head'), may hold values from -80 to 80
- prefix_keys: bfloat16 [16384, 1024], P('ctx', 'head'), may hold values from -8 to 8
- prefix_values: bfloat16 [16384, 1024], P('ctx', 'head'), may hold values from -4 to 4
- dec_query: bfloat16 [64, 5120], P(None, 'head'), may hold values from -80 to 80
- kept_pages: int32 [16, 16, 2], P(None, 'ctx'), may hold values from 0 to 7, as said below
- page_counts: int32 [16, 16], replicated, may hold values from 0 to 2, as said below
- assignment: int32 [64], replicated, may hold values from 0 to 63, each once
Outputs:
- token_scores: float32 [4, 16384], P(None, ('ctx', 'head'))
- decode_out: bfloat16 [64, 5120], P('ctx', 'head')
The draws below stay inside these ranges and needn't reach their ends.
Inputs may be any that keep to these rules, and one draw needn't show every extreme that they name: kept_pages[p, o, j] is the index, among the 8 pages of the context shard at ctx index o, of the page that replica p keeps in slot j; a slot holds a kept page only if j < page_counts[p, o]; the two slots of one p and o name different pages; slot 0 of shard 0 is page 0 for every replica. page_counts[p, o] counts the pages replica p keeps from shard o; it is at least 1 for shard 0, and some replica keeps 2 pages from every shard.
All inputs are finite; a program needn't handle non-finite values.
Results may differ from the reference program's by a relative error of at most 0.0012.
Values may be sent and summed in bfloat16 or wider, within the bound.
A program may use at most 64 MiB of HBM per device.

```python
import math
import jax
import jax.numpy as jnp
from jax import lax

QH = 40
KVH = 8
HD = 128
OBS = 64
POOL = 7
PAGE = 128
CAP = 2
R = 4
SLOTS = 4
G = 5
TOKENS = 16384
PAGES_DEV = 8
REPL = 16
RD = 64


def query_draw(key, row_total, spread, salt):
    noise_key = jax.random.fold_in(jax.random.fold_in(key, salt), 0)
    base = jnp.clip(spread * jax.random.normal(noise_key, (row_total, QH * HD), jnp.float32), -4.0 * spread, 4.0 * spread)
    return base.astype(jnp.bfloat16)


def draw_obs_query(key, part):
    return query_draw(key, R * OBS, 1.0, 31)


def draw_dec_query(key, part):
    return query_draw(key, RD, 2.0, 51)


def draw_prefix_keys(key, part):
    noise_key, scale_key = jax.random.split(jax.random.fold_in(key, 21), 2)
    raw = jnp.clip(jax.random.normal(noise_key, (TOKENS, KVH * HD), jnp.float32), -4.0, 4.0)
    scales = jnp.exp(jax.random.uniform(scale_key, (TOKENS, 1), jnp.float32, math.log(0.4), math.log(2.0)))
    keys_all = raw * scales
    return keys_all.astype(jnp.bfloat16)


def page_layout(key):
    level_key, full_key, coin_key, first_key, step_key = jax.random.split(jax.random.fold_in(key, 41), 5)
    levels = jnp.array([1, 2, 4, 8], jnp.int32)[jax.random.randint(level_key, (REPL,), 0, 4)]
    busiest = jax.random.randint(full_key, (), 0, REPL)
    replica_ids = jnp.arange(REPL)
    levels = jnp.where(replica_ids == busiest, 8, levels)
    coins = jax.random.randint(coin_key, (REPL, REPL, CAP), 0, 8)
    counts = jnp.sum(jnp.where(coins < levels[:, None, None], 1, 0), axis=-1).astype(jnp.int32)
    first_shard = (replica_ids == 0)[None, :]
    counts = jnp.where(first_shard, jnp.maximum(counts, 1), counts).astype(jnp.int32)
    first_page = jax.random.randint(first_key, (REPL, REPL), 0, PAGES_DEV)
    first_page = jnp.where(first_shard, 0, first_page)
    second_page = (first_page + jax.random.randint(step_key, (REPL, REPL), 1, PAGES_DEV)) % PAGES_DEV
    return (jnp.stack([first_page, second_page], axis=-1).astype(jnp.int32), counts)


def draw_kept_pages(key, part):
    return page_layout(key)[0]


def draw_page_counts(key, part):
    return page_layout(key)[1]


def shard_levels(stream_key, extent, pieces, low, largest):
    level = 1.0
    for dim, shards_of in pieces:
        steps = jax.random.uniform(jax.random.fold_in(jax.random.fold_in(stream_key, 6), dim), (shards_of,), jnp.float32, low / len(pieces), largest / len(pieces))
        level = level * jnp.repeat(jnp.exp(steps), extent[dim] // shards_of).reshape((-1,) + (1,) * (len(extent) - 1 - dim))
    return level


def centred(stream_key, shape, scale, bound, cuts=(), held_as=jnp.bfloat16):
    result = scale * jax.random.normal(stream_key, shape, jnp.float32)
    if cuts:
        result = result * shard_levels(stream_key, shape, cuts, -0.22, 0.18)
    return jnp.clip(result, -bound, bound).astype(held_as)


def setup_inputs(seed: int = 0) -> dict:
    arg_keys = jax.random.split(jax.random.key(seed), 8)
    return {
        "obs_query": draw_obs_query(jax.random.fold_in(arg_keys[7], 71), 0),
        "prefix_keys": draw_prefix_keys(jax.random.fold_in(arg_keys[7], 71), 0),
        "prefix_values": centred(arg_keys[2], (TOKENS, KVH * HD), 1.0, 4.0, ((0, 16), (1, 2))),
        "dec_query": draw_dec_query(jax.random.fold_in(arg_keys[7], 71), 0),
        "kept_pages": draw_kept_pages(jax.random.fold_in(arg_keys[7], 71), 0),
        "page_counts": draw_page_counts(jax.random.fold_in(arg_keys[7], 71), 0),
        "assignment": jax.random.permutation(arg_keys[6], RD).astype(jnp.int32),
    }


masked_low = -1e+30

def window_sum(padded, span_len):
    running = padded[:, 0:span_len]
    for offset in range(1, POOL):
        running = running + padded[:, offset:offset + span_len]
    return running

def reference(obs_query, prefix_keys, prefix_values, dec_query, kept_pages, page_counts, assignment):
    score_scale = 1.0 / math.sqrt(HD)
    row_count = R * OBS
    head_queries = obs_query.reshape(row_count, QH, HD)

    def head_step(running, head_idx):
        query_head = lax.dynamic_index_in_dim(head_queries, head_idx, 1, keepdims=False)
        key_head = lax.dynamic_slice_in_dim(prefix_keys, head_idx // G * HD, HD, 1)
        scores = jnp.dot(query_head, key_head.T, preferred_element_type=jnp.float32) * score_scale
        row_max = lax.optimization_barrier(jnp.max(scores, axis=1, keepdims=True))
        raised = jnp.exp(scores - row_max)
        weights = raised / lax.optimization_barrier(jnp.sum(raised, axis=1, keepdims=True))
        return (running + weights.reshape(R, OBS, TOKENS).sum(axis=1), None)
    attended, _ = lax.scan(head_step, jnp.zeros((R, TOKENS), jnp.float32), jnp.arange(QH, dtype=jnp.int32))
    padded = jnp.pad(attended, ((0, 0), (POOL // 2, POOL // 2)))
    token_scores = window_sum(padded, TOKENS) * (TOKENS / (OBS * QH * POOL))
    key_pages = prefix_keys.reshape(TOKENS // PAGE, PAGE, KVH * HD)
    value_pages = prefix_values.reshape(TOKENS // PAGE, PAGE, KVH * HD)
    shard_base = jnp.arange(REPL, dtype=jnp.int32)[:, None] * PAGES_DEV
    slot_index = jnp.arange(CAP, dtype=jnp.int32)

    def replica_step(unused, inputs):
        kept_row, count_row, replica = inputs
        page_ids = (shard_base + kept_row).reshape(-1).astype(jnp.int32)
        token_keys = jnp.take(key_pages, page_ids, axis=0).reshape(REPL * CAP * PAGE, KVH, HD).astype(jnp.float32)
        token_values = jnp.take(value_pages, page_ids, axis=0).reshape(REPL * CAP * PAGE, KVH, HD).astype(jnp.float32)
        live_slots = jnp.broadcast_to((slot_index[None, :] < count_row[:, None])[:, :, None], (REPL, CAP, PAGE)).reshape(-1)
        requests = lax.dynamic_slice_in_dim(assignment, (replica * SLOTS).astype(jnp.int32), SLOTS)
        queries = jnp.take(dec_query, requests, axis=0).reshape(SLOTS, KVH, G, HD).astype(jnp.float32)
        scores = jnp.einsum('skgd,tkd->skgt', queries, token_keys, precision=lax.Precision.HIGHEST) * score_scale
        scores = jnp.where(live_slots, scores, masked_low)
        row_top = lax.optimization_barrier(jnp.max(scores, axis=-1, keepdims=True))
        raised = jnp.where(live_slots, jnp.exp(scores - row_top), 0.0)
        weights = raised / lax.optimization_barrier(jnp.sum(raised, axis=-1, keepdims=True))
        attended_values = jnp.einsum('skgt,tkd->skgd', weights, token_values, precision=lax.Precision.HIGHEST)
        return (unused, attended_values.reshape(SLOTS, QH * HD).astype(jnp.bfloat16))
    _, decoded = lax.scan(replica_step, jnp.zeros((), jnp.float32), (kept_pages, page_counts, jnp.arange(REPL, dtype=jnp.int32)))
    decode_out = decoded.reshape(RD, QH * HD)
    return (token_scores, decode_out)
```

```python
import functools
import math

import jax
import jax.numpy as jnp
from jax import lax
from jax.experimental import pallas as pl
from jax.experimental.pallas import tpu as pltpu
from jax.sharding import PartitionSpec as P

QH = 40
HD = 128
OBS = 64
POOL = 7
PAGE = 128
SLOTS = 4
G = 5
R = 4
LANES = 128

masked_low = -1e30
MESH = pl.DeviceIdType.MESH
NT = (((1,), (1,)), ((), ()))


def nt_dot(a, b):
    return lax.dot_general(a, b, NT, preferred_element_type=jnp.float32)


def split(x):
    hi = x.astype(jnp.bfloat16)
    return hi, (x - hi.astype(jnp.float32)).astype(jnp.bfloat16)


def kernel(
    n, heads, side, rows,
    obs, keys, values, dec_query, aux,
    tok, dec,
    gath, raised, total, qd, dsend, drecv, stat, srecv, fin, weight, wsend, wrecv, esend, erecv,
    o_send, o_recv, d_send, d_recv, s_send, s_recv, f_send, f_recv, w_send, w_recv, e_send, e_recv,
):
    ctx_len = keys.shape[0]
    kv = keys.shape[1] // HD
    hl = kv * G
    reqs = dec_query.shape[0]
    q_rows = n * rows
    padded_rows = obs.shape[0]
    halves = q_rows // LANES
    chunk_rows = stat.shape[1] // 2
    scale = 1.0 / math.sqrt(HD)
    scale2 = scale * math.log2(math.e)
    me = lax.axis_index("ctx")
    core = lax.axis_index("head")
    major, minor = me // side, me % side
    last = n - 1

    barrier = pltpu.get_barrier_semaphore()

    def greet(who):
        pl.semaphore_signal(barrier, inc=1, device_id=who, device_id_type=MESH)

    @pl.loop(1, n)
    def _(d):
        greet((lax.rem(me + d, n), core))

    for d in range(1, heads):
        other = lax.rem(core + d, heads)
        greet((me, other))

        @pl.when(me > 0)
        def _():
            greet((me - 1, other))

        @pl.when(me < last)
        def _():
            greet((me + 1, other))

    near = jnp.where(me > 0, 1, 0) + jnp.where(me < last, 1, 0)
    pl.semaphore_wait(barrier, n - 1 + (heads - 1) * (1 + near))

    def obs_copy(source, slot, to, sem):
        return pltpu.make_async_remote_copy(
            src_ref=source, dst_ref=gath.at[slot], send_sem=o_send.at[sem],
            recv_sem=o_recv.at[slot], device_id=(to, core), device_id_type=MESH,
        )

    def column(d):
        return lax.rem(major + d, side) * side + minor

    def across(d):
        return major * side + lax.rem(minor + d, side)

    for d in range(1, side):
        obs_copy(obs, me, column(d), d).start()
    for d in range(1, side):
        obs_copy(obs, me, across(d), d * side).start()
    gath[me] = obs[...]

    pick = jnp.where(
        aux[:, 0:1] == lax.broadcasted_iota(jnp.int32, (reqs, reqs), 1), 1.0, 0.0
    ).astype(jnp.bfloat16)
    for k in range(kv):
        cols = pl.ds(k * G * HD, G * HD)
        qd[:, cols] = jnp.dot(
            pick, dec_query[:, cols], preferred_element_type=jnp.float32
        ).astype(jnp.bfloat16)
    page = lax.broadcasted_iota(jnp.int32, (reqs, ctx_len), 1) // PAGE
    bias = jnp.where((page == aux[:, 1:2]) | (page == aux[:, 2:3]), 0.0, masked_low)
    bias = jnp.concatenate([bias] * G, axis=0)
    lane = lax.broadcasted_iota(jnp.int32, (reqs, LANES), 1)

    maxima = jnp.zeros((reqs, LANES), jnp.float32)
    sums = jnp.zeros((reqs, LANES), jnp.float32)
    for k in range(kv):
        q = jnp.concatenate([qd[:, pl.ds((k * G + g) * HD, HD)] for g in range(G)], axis=0)
        s = nt_dot(q, keys[:, pl.ds(k * HD, HD)]) * scale + bias
        top = jnp.max(s, axis=1, keepdims=True)
        e = jnp.exp(s - top)
        amount = jnp.sum(e, axis=1, keepdims=True)
        hi, lo = split(e)
        v = values[:, pl.ds(k * HD, HD)]
        acc = jnp.dot(hi, v, preferred_element_type=jnp.float32) + jnp.dot(
            lo, v, preferred_element_type=jnp.float32
        )
        for g in range(G):
            h = k * G + g
            part = slice(g * reqs, (g + 1) * reqs)
            maxima = jnp.where(lane == h, top[part], maxima)
            sums = jnp.where(lane == h, amount[part], sums)
            for p in range(n):
                at = g * reqs + p * SLOTS
                dsend[p, h] = acc[at : at + SLOTS]
        if k == 0:
            for d in range(1, side):
                slot = column(d)
                obs_copy(obs, slot, me, d).wait_recv()
                for f in range(1, side):
                    obs_copy(gath.at[slot], slot, across(f), f * side + d).start()
    for p in range(n):
        dsend[p, hl] = maxima[p * SLOTS : (p + 1) * SLOTS]
        dsend[p, hl + 1] = sums[p * SLOTS : (p + 1) * SLOTS]

    def spread(source, target, send, recv):
        def copy(d):
            to = lax.rem(me + d, n)
            return pltpu.make_async_remote_copy(
                src_ref=source(to), dst_ref=target.at[me], send_sem=send.at[d],
                recv_sem=recv.at[me], device_id=(to, core), device_id_type=MESH,
            )

        def arrival(d):
            frm = lax.rem(me + n - d, n)
            return pltpu.make_async_remote_copy(
                src_ref=source(frm), dst_ref=target.at[frm], send_sem=send.at[d],
                recv_sem=recv.at[frm], device_id=(frm, core), device_id_type=MESH,
            )

        def start():
            @pl.loop(1, n)
            def _(d):
                copy(d).start()

        def finish():
            @pl.loop(1, n)
            def _(d):
                arrival(d).wait_recv()

        def drain():
            @pl.loop(1, n)
            def _(d):
                copy(d).wait_send()

        return start, finish, drain

    d_start, d_finish, d_drain = spread(lambda to: dsend.at[to], drecv, d_send, d_recv)
    s_start, s_finish, s_drain = spread(lambda to: stat.at[to], srecv, s_send, s_recv)
    f_start, f_finish, f_drain = spread(lambda to: fin.at[me], fin, f_send, f_recv)
    d_start()
    drecv[me] = dsend[me]

    for f in range(1, side):
        for d in range(side):
            slot = lax.rem(major + d, side) * side + lax.rem(minor + f, side)
            obs_copy(obs, slot, me, d).wait_recv()

    stat[...] = jnp.zeros_like(stat)

    @pl.loop(0, hl)
    def _(h):
        cols = pl.ds(pl.multiple_of(h * HD, HD), HD)
        q = gath[:, :, cols].reshape(n * padded_rows, HD)
        if padded_rows != rows:
            shape = (q_rows, n * padded_rows)
            row = lax.broadcasted_iota(jnp.int32, shape, 0)
            col = lax.broadcasted_iota(jnp.int32, shape, 1)
            keep = (row // rows) * padded_rows + row % rows == col
            q = jnp.dot(
                jnp.where(keep, 1.0, 0.0).astype(jnp.bfloat16), q,
                preferred_element_type=jnp.float32,
            ).astype(jnp.bfloat16)
        s = nt_dot(keys[:, pl.ds(pl.multiple_of((h // G) * HD, HD), HD)], q)
        top = jnp.max(s, axis=0, keepdims=True)
        e = jnp.exp2((s - top) * scale2)
        raised[h] = e
        amount = jnp.sum(e, axis=0, keepdims=True)
        for half in range(halves):
            at = h * halves + half
            part = slice(half * LANES, (half + 1) * LANES)
            stat[at // chunk_rows, pl.ds(at % chunk_rows, 1), :] = top[:, part]
            stat[at // chunk_rows, pl.ds(chunk_rows + at % chunk_rows, 1), :] = amount[:, part]

    s_start()
    srecv[me] = stat[me]
    s_finish()
    tops = [srecv[i, 0:chunk_rows, :] for i in range(n)]
    joint = functools.reduce(jnp.maximum, tops)
    gross = jnp.zeros_like(joint)
    for i in range(n):
        gross = gross + srecv[i, chunk_rows : 2 * chunk_rows, :] * jnp.exp2(
            (tops[i] - joint) * scale2
        )
    fin[me] = jnp.concatenate([joint, gross], axis=0)
    f_start()

    d_finish()
    joint_max = drecv[0, hl]
    for i in range(1, n):
        joint_max = jnp.maximum(joint_max, drecv[i, hl])
    factors = [jnp.exp(drecv[i, hl] - joint_max) for i in range(n)]
    running = factors[0] * drecv[0, hl + 1]
    for i in range(1, n):
        running = running + factors[i] * drecv[i, hl + 1]
    inverse = 1.0 / running
    factors = [f * inverse for f in factors]
    for h in range(hl):
        out = factors[0][:, h : h + 1] * drecv[0, h]
        for i in range(1, n):
            out = out + factors[i][:, h : h + 1] * drecv[i, h]
        dec[:, pl.ds(h * HD, HD)] = out.astype(jnp.bfloat16)

    f_finish()

    @pl.loop(0, hl)
    def _(h):
        for half in range(halves):
            at = h * halves + half
            own, low = at // chunk_rows, at % chunk_rows
            mine = stat[own, pl.ds(low, 1), :]
            whole = fin[own, pl.ds(low, 1), :]
            amount = fin[own, pl.ds(chunk_rows + low, 1), :]
            weight[h, :, pl.ds(half * LANES, LANES)] = jnp.exp2((mine - whole) * scale2) / amount

    block = 64

    @pl.loop(0, ctx_len // block)
    def _(b):
        at = pl.ds(pl.multiple_of(b * block, block), block)

        def add(h, acc):
            return acc + raised[h, at, :] * weight[h]

        total[at, :] = lax.fori_loop(
            0, hl, add, jnp.zeros((block, q_rows), jnp.float32), unroll=True
        )

    request = lax.broadcasted_iota(jnp.int32, (8, q_rows), 1) // OBS
    fold = jnp.where(request == lax.broadcasted_iota(jnp.int32, (8, q_rows), 0), 1.0, 0.0)
    fold = fold.astype(jnp.bfloat16)
    hi, lo = split(total[...])
    attended = nt_dot(fold, hi) + nt_dot(fold, lo)
    zeros = jnp.zeros((8, LANES), jnp.float32)
    wide = jnp.concatenate([zeros, attended, zeros], axis=1)
    width = ctx_len + 2 * LANES
    pooled = wide
    for d in range(1, POOL // 2 + 1):
        pooled = pooled + pltpu.roll(wide, d, 1) + pltpu.roll(wide, width - d, 1)
    pooled = pooled * (ctx_len * n / (OBS * QH * POOL))
    span = ctx_len // heads
    for j in range(heads):
        wsend[j] = pooled[:, LANES + j * span : LANES + (j + 1) * span]
    esend[0] = pooled[:, :LANES]
    esend[1] = pooled[:, LANES + ctx_len :]

    def w_copy(d, to):
        return pltpu.make_async_remote_copy(
            src_ref=wsend.at[to], dst_ref=wrecv.at[core], send_sem=w_send.at[d],
            recv_sem=w_recv.at[core], device_id=(me, to), device_id_type=MESH,
        )

    def w_arrival(frm):
        return pltpu.make_async_remote_copy(
            src_ref=wsend.at[frm], dst_ref=wrecv.at[frm], send_sem=w_send.at[0],
            recv_sem=w_recv.at[frm], device_id=(me, frm), device_id_type=MESH,
        )

    def e_copy(side_of, to_ctx, to_core, slot):
        return pltpu.make_async_remote_copy(
            src_ref=esend.at[side_of], dst_ref=erecv.at[slot], send_sem=e_send.at[side_of],
            recv_sem=e_recv.at[slot], device_id=(to_ctx, to_core), device_id_type=MESH,
        )

    @pl.when(me > 0)
    def _():
        e_copy(0, me - 1, heads - 1, core).start()

    @pl.when(me < last)
    def _():
        e_copy(1, me + 1, 0, core).start()

    for d in range(1, heads):
        w_copy(d, lax.rem(core + d, heads)).start()
    wrecv[core] = wsend[core]
    for d in range(1, heads):
        w_arrival(lax.rem(core + d, heads)).wait_recv()
    result = wrecv[0]
    for j in range(1, heads):
        result = result + wrecv[j]
    tok[...] = result[:R]

    def edge():
        for j in range(heads):
            e_copy(0, me, core, j).wait_recv()
        rim = erecv[0]
        for j in range(1, heads):
            rim = rim + erecv[j]
        return rim[:R]

    @pl.when((core == 0) & (me > 0))
    def _():
        tok[:, 0:LANES] = tok[:, 0:LANES] + edge()

    @pl.when((core == heads - 1) & (me < last))
    def _():
        tok[:, span - LANES : span] = tok[:, span - LANES : span] + edge()

    for d in range(1, side):
        obs_copy(obs, me, column(d), d).wait_send()
        obs_copy(obs, me, across(d), d * side).wait_send()
        for f in range(1, side):
            slot = column(d)
            obs_copy(gath.at[slot], slot, across(f), f * side + d).wait_send()
    d_drain()
    s_drain()
    f_drain()
    for d in range(1, heads):
        w_copy(d, lax.rem(core + d, heads)).wait_send()

    @pl.when(me > 0)
    def _():
        e_copy(0, me - 1, heads - 1, core).wait_send()

    @pl.when(me < last)
    def _():
        e_copy(1, me + 1, 0, core).wait_send()


def local(n, heads, obs_query, prefix_keys, prefix_values, dec_query, kept_pages, page_counts, assignment):
    rows, width = obs_query.shape
    ctx_len = prefix_keys.shape[0]
    hl = width // HD
    reqs = dec_query.shape[0]
    q_rows = n * rows
    side = math.isqrt(n)
    while n % side:
        side -= 1
    padded_rows = -(-rows // 16) * 16
    obs = jnp.pad(obs_query, ((0, padded_rows - rows), (0, 0)))
    counts = lax.dynamic_index_in_dim(page_counts, lax.axis_index("ctx"), 1, keepdims=True)
    cap = kept_pages.shape[2]
    live = jnp.arange(cap, dtype=jnp.int32)[None, :] < counts
    kept = jnp.where(live, kept_pages[:, 0, :], -1)
    aux = jnp.concatenate([assignment[:, None], jnp.repeat(kept, SLOTS, axis=0)], axis=1)
    chunk_rows = -(-(hl * q_rows // LANES) // n)
    f32 = jnp.float32
    span = ctx_len // heads
    dma = pltpu.SemaphoreType.DMA
    vmem = pl.BlockSpec(memory_space=pltpu.VMEM)
    return pl.pallas_call(
        functools.partial(kernel, n, heads, side, rows),
        out_shape=(
            jax.ShapeDtypeStruct((R, span), f32),
            jax.ShapeDtypeStruct((SLOTS, width), jnp.bfloat16),
        ),
        in_specs=[vmem] * 5,
        out_specs=(vmem, vmem),
        scratch_shapes=[
            pltpu.VMEM((n, padded_rows, width), jnp.bfloat16),
            pltpu.VMEM((hl, ctx_len, q_rows), f32),
            pltpu.VMEM((ctx_len, q_rows), f32),
            pltpu.VMEM((reqs, width), jnp.bfloat16),
            pltpu.VMEM((n, hl + 2, SLOTS, LANES), f32),
            pltpu.VMEM((n, hl + 2, SLOTS, LANES), f32),
            pltpu.VMEM((n, 2 * chunk_rows, LANES), f32),
            pltpu.VMEM((n, 2 * chunk_rows, LANES), f32),
            pltpu.VMEM((n, 2 * chunk_rows, LANES), f32),
            pltpu.VMEM((hl, 1, q_rows), f32),
            pltpu.VMEM((heads, 8, span), f32),
            pltpu.VMEM((heads, 8, span), f32),
            pltpu.VMEM((2, 8, LANES), f32),
            pltpu.VMEM((heads, 8, LANES), f32),
            dma((side * side,)), dma((n,)),
            dma((n,)), dma((n,)),
            dma((n,)), dma((n,)),
            dma((n,)), dma((n,)),
            dma((heads,)), dma((heads,)),
            dma((2,)), dma((heads,)),
        ],
        compiler_params=pltpu.CompilerParams(
            collective_id=0, has_side_effects=True, vmem_limit_bytes=50 * 1024 * 1024
        ),
        cost_estimate=pl.CostEstimate(
            flops=4 * hl * q_rows * ctx_len * HD, bytes_accessed=4 * ctx_len * width,
            transcendentals=hl * q_rows * ctx_len,
        ),
    )(obs, prefix_keys, prefix_values, dec_query, aux)


def solution(mesh):
    in_specs = (
        P("ctx", "head"),
        P("ctx", "head"),
        P("ctx", "head"),
        P(None, "head"),
        P(None, "ctx", None),
        P(),
        P(),
    )
    out_specs = (P(None, ("ctx", "head")), P("ctx", "head"))
    body = functools.partial(local, mesh.shape["ctx"], mesh.shape["head"])
    return jax.shard_map(body, mesh=mesh, in_specs=in_specs, out_specs=out_specs, check_vma=False)
```

```python
import functools
import math

import jax
import jax.numpy as jnp
from jax import lax
from jax.experimental import pallas as pl
from jax.experimental.pallas import tpu as pltpu
from jax.sharding import PartitionSpec as P

QH = 40
HD = 128
OBS = 64
POOL = 7
PAGE = 128
SLOTS = 4
G = 5
R = 4
LANES = 128
EARLY = 0

masked_low = -1e30
MESH = pl.DeviceIdType.MESH
NT = (((1,), (1,)), ((), ()))


def nt_dot(a, b):
    return lax.dot_general(a, b, NT, preferred_element_type=jnp.float32)


def split(x):
    hi = x.astype(jnp.bfloat16)
    return hi, (x - hi.astype(jnp.float32)).astype(jnp.bfloat16)


def kernel(
    n, heads, side, rows,
    obs, keys_in, values_in, dec_query_in, assign, kept, counts,
    tok, dec,
    keys, values, dec_query, gath, raised, total, qd, dsend, drecv, stat, srecv, fin, weight, wsend, wrecv, esend, erecv,
    o_send, o_recv, d_send, d_recv, s_send, s_recv, f_send, f_recv, w_send, w_recv, e_send, e_recv, l_sem,
):
    ctx_len = keys.shape[0]
    kv = keys.shape[1] // HD
    hl = kv * G
    reqs = dec_query.shape[0]
    q_rows = n * rows
    padded_rows = obs.shape[0]
    halves = q_rows // LANES
    chunk_rows = stat.shape[1] // 2
    scale = 1.0 / math.sqrt(HD)
    scale2 = scale * math.log2(math.e)
    me = lax.axis_index("ctx")
    core = lax.axis_index("head")
    major, minor = me // side, me % side
    last = n - 1

    barrier = pltpu.get_barrier_semaphore()

    def greet(who):
        pl.semaphore_signal(barrier, inc=1, device_id=who, device_id_type=MESH)

    @pl.loop(1, n)
    def _(d):
        greet((lax.rem(me + d, n), core))

    for d in range(1, heads):
        other = lax.rem(core + d, heads)
        greet((me, other))

        @pl.when(me > 0)
        def _():
            greet((me - 1, other))

        @pl.when(me < last)
        def _():
            greet((me + 1, other))

    loads = [
        pltpu.make_async_copy(dec_query_in, dec_query, l_sem.at[0]),
        pltpu.make_async_copy(keys_in, keys, l_sem.at[1]),
        pltpu.make_async_copy(values_in, values, l_sem.at[2]),
    ]
    for load in loads:
        load.start()

    near = jnp.where(me > 0, 1, 0) + jnp.where(me < last, 1, 0)
    def obs_copy(source, slot, to, sem):
        return pltpu.make_async_remote_copy(
            src_ref=source, dst_ref=gath.at[slot], send_sem=o_send.at[sem],
            recv_sem=o_recv.at[slot], device_id=(to, core), device_id_type=MESH,
        )

    def column(d):
        return lax.rem(major + d, side) * side + minor

    def across(d):
        return major * side + lax.rem(minor + d, side)

    gath[me] = obs[...]
    owner = lax.broadcasted_iota(jnp.int32, (reqs, n), 0) // SLOTS
    source = lax.broadcasted_iota(jnp.int32, (reqs, n), 1)
    mine = owner == source
    count = jnp.dot(
        jnp.where(mine, 1.0, 0.0).astype(jnp.bfloat16),
        counts[...].astype(jnp.float32).astype(jnp.bfloat16),
        preferred_element_type=jnp.float32,
    )
    count = jnp.sum(jnp.where(source == me, count, 0.0), axis=1, keepdims=True)
    page = lax.broadcasted_iota(jnp.int32, (reqs, ctx_len), 1) // PAGE
    page = page.astype(jnp.float32)
    bias = jnp.full((reqs, ctx_len), masked_low, jnp.float32)
    for j in range(kept.shape[0]):
        slot_page = jnp.where(mine, kept[j : j + 1, :].astype(jnp.float32), 0.0)
        slot_page = jnp.sum(slot_page, axis=1, keepdims=True)
        slot_page = jnp.where(count > j, slot_page, -1.0)
        bias = jnp.where(page == slot_page, 0.0, bias)
    bias = jnp.concatenate([bias] * G, axis=0)
    lane = lax.broadcasted_iota(jnp.int32, (reqs, LANES), 1)
    pick = jnp.where(
        assign[...] == lax.broadcasted_iota(jnp.int32, (reqs, reqs), 0), 1.0, 0.0
    ).astype(jnp.bfloat16)
    loads[0].wait()
    for k in range(kv):
        cols = pl.ds(k * G * HD, G * HD)
        qd[:, cols] = lax.dot_general(
            pick, dec_query[:, cols], (((0,), (0,)), ((), ())),
            preferred_element_type=jnp.float32,
        ).astype(jnp.bfloat16)
    loads[1].wait()
    loads[2].wait()

    maxima = jnp.zeros((reqs, LANES), jnp.float32)
    sums = jnp.zeros((reqs, LANES), jnp.float32)

    def forward(m):
        slot = m * side + minor

        @pl.when(major != m)
        def _():
            obs_copy(obs, slot, me, 0).wait_recv()

        for f in range(1, side):
            obs_copy(gath.at[slot], slot, across(f), f * side + m).start()

    ahead = min(EARLY, kv - 1)
    for k in range(kv):
        if k == ahead:
            pl.semaphore_wait(barrier, n - 1 + (heads - 1) * (1 + near))
            for d in range(1, side):
                obs_copy(obs, me, column(d), d).start()
        q = jnp.concatenate([qd[:, pl.ds((k * G + g) * HD, HD)] for g in range(G)], axis=0)
        s = nt_dot(q, keys[:, pl.ds(k * HD, HD)]) * scale + bias
        top = jnp.max(s, axis=1, keepdims=True)
        e = jnp.exp(s - top)
        amount = jnp.sum(e, axis=1, keepdims=True)
        hi, lo = split(e)
        v = values[:, pl.ds(k * HD, HD)]
        acc = jnp.dot(hi, v, preferred_element_type=jnp.float32) + jnp.dot(
            lo, v, preferred_element_type=jnp.float32
        )
        for g in range(G):
            h = k * G + g
            part = slice(g * reqs, (g + 1) * reqs)
            maxima = jnp.where(lane == h, top[part], maxima)
            sums = jnp.where(lane == h, amount[part], sums)
            for p in range(n):
                at = g * reqs + p * SLOTS
                dsend[p, h] = acc[at : at + SLOTS]
        if k > ahead:
            forward(k - ahead - 1)
    for m in range(kv - ahead - 1, side):
        forward(m)
    for p in range(n):
        dsend[p, hl] = maxima[p * SLOTS : (p + 1) * SLOTS]
        dsend[p, hl + 1] = sums[p * SLOTS : (p + 1) * SLOTS]

    def spread(source, target, send, recv):
        def copy(d):
            to = lax.rem(me + d, n)
            return pltpu.make_async_remote_copy(
                src_ref=source(to), dst_ref=target.at[me], send_sem=send.at[d],
                recv_sem=recv.at[me], device_id=(to, core), device_id_type=MESH,
            )

        def arrival(d):
            frm = lax.rem(me + n - d, n)
            return pltpu.make_async_remote_copy(
                src_ref=source(frm), dst_ref=target.at[frm], send_sem=send.at[d],
                recv_sem=recv.at[frm], device_id=(frm, core), device_id_type=MESH,
            )

        def start():
            @pl.loop(1, n)
            def _(d):
                copy(d).start()

        def finish():
            @pl.loop(1, n)
            def _(d):
                arrival(d).wait_recv()

        def drain():
            @pl.loop(1, n)
            def _(d):
                copy(d).wait_send()

        return start, finish, drain

    d_start, d_finish, d_drain = spread(lambda to: dsend.at[to], drecv, d_send, d_recv)
    s_start, s_finish, s_drain = spread(lambda to: stat.at[to], srecv, s_send, s_recv)
    f_start, f_finish, f_drain = spread(lambda to: fin.at[me], fin, f_send, f_recv)
    drecv[me] = dsend[me]
    stat[...] = jnp.zeros_like(stat)
    per_half = n // halves
    majors_half = side // halves

    for half in range(halves):
        for m in range(half * majors_half, (half + 1) * majors_half):
            for f in range(1, side):
                slot = m * side + lax.rem(minor + f, side)
                obs_copy(obs, slot, me, 0).wait_recv()
        if half == halves - 1:
            d_start()

        @pl.loop(0, hl, unroll=2)
        def _(h):
            cols = pl.ds(pl.multiple_of(h * HD, HD), HD)
            q = gath[half * per_half : (half + 1) * per_half, :, cols]
            q = q.reshape(per_half * padded_rows, HD)
            if padded_rows != rows:
                shape = (LANES, per_half * padded_rows)
                row = lax.broadcasted_iota(jnp.int32, shape, 0)
                col = lax.broadcasted_iota(jnp.int32, shape, 1)
                keep = (row // rows) * padded_rows + row % rows == col
                q = jnp.dot(
                    jnp.where(keep, 1.0, 0.0).astype(jnp.bfloat16), q,
                    preferred_element_type=jnp.float32,
                ).astype(jnp.bfloat16)
            s = nt_dot(keys[:, pl.ds(pl.multiple_of((h // G) * HD, HD), HD)], q)
            top = jnp.max(s, axis=0, keepdims=True)
            e = jnp.exp2((s - top) * scale2)
            raised[half, h] = e
            at = h * halves + half
            stat[at // chunk_rows, pl.ds(at % chunk_rows, 1), :] = top
            stat[at // chunk_rows, pl.ds(chunk_rows + at % chunk_rows, 1), :] = jnp.sum(
                e, axis=0, keepdims=True
            )

    s_start()
    srecv[me] = stat[me]
    s_finish()
    tops = [srecv[i, 0:chunk_rows, :] for i in range(n)]
    joint = functools.reduce(jnp.maximum, tops)
    gross = jnp.zeros_like(joint)
    for i in range(n):
        gross = gross + srecv[i, chunk_rows : 2 * chunk_rows, :] * jnp.exp2(
            (tops[i] - joint) * scale2
        )
    fin[me] = jnp.concatenate([joint, gross], axis=0)
    f_start()

    d_finish()
    joint_max = drecv[0, hl]
    for i in range(1, n):
        joint_max = jnp.maximum(joint_max, drecv[i, hl])
    factors = [jnp.exp(drecv[i, hl] - joint_max) for i in range(n)]
    running = factors[0] * drecv[0, hl + 1]
    for i in range(1, n):
        running = running + factors[i] * drecv[i, hl + 1]
    inverse = 1.0 / running
    factors = [f * inverse for f in factors]
    for h in range(hl):
        out = factors[0][:, h : h + 1] * drecv[0, h]
        for i in range(1, n):
            out = out + factors[i][:, h : h + 1] * drecv[i, h]
        dec[:, pl.ds(h * HD, HD)] = out.astype(jnp.bfloat16)

    f_finish()

    @pl.loop(0, hl)
    def _(h):
        for half in range(halves):
            at = h * halves + half
            own, low = at // chunk_rows, at % chunk_rows
            mine = stat[own, pl.ds(low, 1), :]
            whole = fin[own, pl.ds(low, 1), :]
            amount = fin[own, pl.ds(chunk_rows + low, 1), :]
            weight[half, h] = jnp.exp2((mine - whole) * scale2) / amount

    block = 128

    for half in range(halves):

        @pl.loop(0, ctx_len // block)
        def _(b):
            at = pl.ds(pl.multiple_of(b * block, block), block)

            def add(h, acc):
                return acc + raised[half, h, at, :] * weight[half, h]

            total[at, half * LANES : (half + 1) * LANES] = lax.fori_loop(
                0, hl, add, jnp.zeros((block, LANES), jnp.float32), unroll=True
            )

    request = lax.broadcasted_iota(jnp.int32, (8, q_rows), 1) // OBS
    fold = jnp.where(request == lax.broadcasted_iota(jnp.int32, (8, q_rows), 0), 1.0, 0.0)
    fold = fold.astype(jnp.bfloat16)
    hi, lo = split(total[...])
    attended = nt_dot(fold, hi) + nt_dot(fold, lo)
    zeros = jnp.zeros((8, LANES), jnp.float32)
    wide = jnp.concatenate([zeros, attended, zeros], axis=1)
    width = ctx_len + 2 * LANES
    pooled = wide
    for d in range(1, POOL // 2 + 1):
        pooled = pooled + pltpu.roll(wide, d, 1) + pltpu.roll(wide, width - d, 1)
    pooled = pooled * (ctx_len * n / (OBS * QH * POOL))
    span = ctx_len // heads
    for j in range(heads):
        wsend[j] = pooled[:, LANES + j * span : LANES + (j + 1) * span]
    esend[0] = pooled[:, :LANES]
    esend[1] = pooled[:, LANES + ctx_len :]

    def w_copy(d, to):
        return pltpu.make_async_remote_copy(
            src_ref=wsend.at[to], dst_ref=wrecv.at[core], send_sem=w_send.at[d],
            recv_sem=w_recv.at[core], device_id=(me, to), device_id_type=MESH,
        )

    def w_arrival(frm):
        return pltpu.make_async_remote_copy(
            src_ref=wsend.at[frm], dst_ref=wrecv.at[frm], send_sem=w_send.at[0],
            recv_sem=w_recv.at[frm], device_id=(me, frm), device_id_type=MESH,
        )

    def e_copy(side_of, to_ctx, to_core, slot):
        return pltpu.make_async_remote_copy(
            src_ref=esend.at[side_of], dst_ref=erecv.at[slot], send_sem=e_send.at[side_of],
            recv_sem=e_recv.at[slot], device_id=(to_ctx, to_core), device_id_type=MESH,
        )

    @pl.when(me > 0)
    def _():
        e_copy(0, me - 1, heads - 1, core).start()

    @pl.when(me < last)
    def _():
        e_copy(1, me + 1, 0, core).start()

    for d in range(1, heads):
        w_copy(d, lax.rem(core + d, heads)).start()
    wrecv[core] = wsend[core]
    for d in range(1, heads):
        w_arrival(lax.rem(core + d, heads)).wait_recv()
    result = wrecv[0]
    for j in range(1, heads):
        result = result + wrecv[j]
    tok[...] = result[:R]

    def edge():
        for j in range(heads):
            e_copy(0, me, core, j).wait_recv()
        rim = erecv[0]
        for j in range(1, heads):
            rim = rim + erecv[j]
        return rim[:R]

    @pl.when((core == 0) & (me > 0))
    def _():
        tok[:, 0:LANES] = tok[:, 0:LANES] + edge()

    @pl.when((core == heads - 1) & (me < last))
    def _():
        tok[:, span - LANES : span] = tok[:, span - LANES : span] + edge()

    for d in range(1, side):
        obs_copy(obs, me, column(d), d).wait_send()
    for m in range(side):
        for f in range(1, side):
            slot = m * side + minor
            obs_copy(gath.at[slot], slot, across(f), f * side + m).wait_send()
    d_drain()
    s_drain()
    f_drain()
    for d in range(1, heads):
        w_copy(d, lax.rem(core + d, heads)).wait_send()

    @pl.when(me > 0)
    def _():
        e_copy(0, me - 1, heads - 1, core).wait_send()

    @pl.when(me < last)
    def _():
        e_copy(1, me + 1, 0, core).wait_send()


def local(n, heads, obs_query, prefix_keys, prefix_values, dec_query, kept_pages, page_counts, assignment):
    rows, width = obs_query.shape
    ctx_len = prefix_keys.shape[0]
    hl = width // HD
    reqs = dec_query.shape[0]
    q_rows = n * rows
    side = math.isqrt(n)
    while n % side:
        side -= 1
    padded_rows = -(-rows // 16) * 16
    obs = jnp.pad(obs_query, ((0, padded_rows - rows), (0, 0)))
    kept = jnp.transpose(kept_pages, (1, 2, 0)).reshape(kept_pages.shape[2], n)
    assign = assignment.reshape(1, reqs)
    chunk_rows = -(-(hl * q_rows // LANES) // n)
    f32 = jnp.float32
    span = ctx_len // heads
    dma = pltpu.SemaphoreType.DMA
    vmem = pl.BlockSpec(memory_space=pltpu.VMEM)
    return pl.pallas_call(
        functools.partial(kernel, n, heads, side, rows),
        out_shape=(
            jax.ShapeDtypeStruct((R, span), f32),
            jax.ShapeDtypeStruct((SLOTS, width), jnp.bfloat16),
        ),
        in_specs=[vmem] + [pl.BlockSpec(memory_space=pl.ANY)] * 3 + [vmem] * 3,
        out_specs=(vmem, vmem),
        scratch_shapes=[
            pltpu.VMEM(prefix_keys.shape, jnp.bfloat16),
            pltpu.VMEM(prefix_values.shape, jnp.bfloat16),
            pltpu.VMEM(dec_query.shape, jnp.bfloat16),
            pltpu.VMEM((n, padded_rows, width), jnp.bfloat16),
            pltpu.VMEM((q_rows // LANES, hl, ctx_len, LANES), f32),
            pltpu.VMEM((ctx_len, q_rows), f32),
            pltpu.VMEM((reqs, width), jnp.bfloat16),
            pltpu.VMEM((n, hl + 2, SLOTS, LANES), f32),
            pltpu.VMEM((n, hl + 2, SLOTS, LANES), f32),
            pltpu.VMEM((n, 2 * chunk_rows, LANES), f32),
            pltpu.VMEM((n, 2 * chunk_rows, LANES), f32),
            pltpu.VMEM((n, 2 * chunk_rows, LANES), f32),
            pltpu.VMEM((q_rows // LANES, hl, 1, LANES), f32),
            pltpu.VMEM((heads, 8, span), f32),
            pltpu.VMEM((heads, 8, span), f32),
            pltpu.VMEM((2, 8, LANES), f32),
            pltpu.VMEM((heads, 8, LANES), f32),
            dma((side * side,)), dma((n,)),
            dma((n,)), dma((n,)),
            dma((n,)), dma((n,)),
            dma((n,)), dma((n,)),
            dma((heads,)), dma((heads,)),
            dma((2,)), dma((heads,)),
            dma((3,)),
        ],
        compiler_params=pltpu.CompilerParams(
            collective_id=0, has_side_effects=True, vmem_limit_bytes=62 * 1024 * 1024
        ),
        cost_estimate=pl.CostEstimate(
            flops=4 * hl * q_rows * ctx_len * HD, bytes_accessed=4 * ctx_len * width,
            transcendentals=hl * q_rows * ctx_len,
        ),
    )(obs, prefix_keys, prefix_values, dec_query, assign, kept, page_counts)


def solution(mesh):
    in_specs = (
        P("ctx", "head"),
        P("ctx", "head"),
        P("ctx", "head"),
        P(None, "head"),
        P(None, "ctx", None),
        P(),
        P(),
    )
    out_specs = (P(None, ("ctx", "head")), P("ctx", "head"))
    body = functools.partial(local, mesh.shape["ctx"], mesh.shape["head"])
    return jax.shard_map(body, mesh=mesh, in_specs=in_specs, out_specs=out_specs, check_vma=False)
```
